32 devices in a mesh: replica: 16 (over z, y, x), shard: 2 (over core).
Axes of the slice: x: 2, y: 2, z: 4, core: 2. Of those that a mesh axis runs over, the one named last changes fastest.
Arguments:
- layer_input: bfloat16 [16384, 960], P(('replica', 'shard')), may hold values from -6 to 6
- segment_ids: int32 [32, 512], P(('replica', 'shard')), may hold values from 0 to 2, never falling along the last dimension, each value on 1 to 384 neighbouring positions
- upstream_grad: bfloat16 [16384, 960], P(('replica', 'shard')), may hold values from -6 to 6
- attn_gain: bfloat16 [960], P('shard'), may hold values from 0.5 to 1.5
- query_weight: bfloat16 [960, 960], P('shard'), may hold values from -0.1875 to 0.1875
- key_weight: bfloat16 [960, 320], P('shard'), may hold values from -0.1875 to 0.1875
- value_weight: bfloat16 [960, 320], P('shard'), may hold values from -0.1875 to 0.1875
- output_weight: bfloat16 [960, 960], P('shard'), may hold values from -2 to 2
- ffn_gain: bfloat16 [960], P('shard'), may hold values from 0.5 to 1.5
- gate_weight: bfloat16 [960, 2560], P(None, 'shard'), may hold values from -0.1875 to 0.1875
- up_weight: bfloat16 [960, 2560], P(None, 'shard'), may hold values from -0.1875 to 0.1875
- down_weight: bfloat16 [2560, 960], P('shard'), may hold values from -0.125 to 0.125
Outputs:
- layer_output: bfloat16 [16384, 960], P(('replica', 'shard'))
- input_grad: float32 [16384, 960], P(('replica', 'shard'))
- attn_gain_grad: float32 [960], P('shard')
- query_weight_grad: float32 [960, 960], P('shard')
- key_weight_grad: float32 [960, 320], P('shard')
- value_weight_grad: float32 [960, 320], P('shard')
- output_weight_grad: float32 [960, 960], P('shard')
- ffn_gain_grad: float32 [960], P('shard')
- gate_weight_grad: float32 [960, 2560], P(None, 'shard')
- up_weight_grad: float32 [960, 2560], P(None, 'shard')
- down_weight_grad: float32 [2560, 960], P('shard')
The draws below stay inside these ranges and needn't reach their ends.
Inputs may be any that keep to these rules, and one draw needn't show every extreme that they name: `segment_ids`: in each row the numbers never fall, every one of 0 to 2 appears, and some document in every draw is 384 tokens long.
All inputs are finite; a program needn't handle non-finite values.
Results may differ from the reference program's by a relative error of at most 0.02.
Values may be sent and summed in bfloat16 or wider, within the bound.
A program may use at most 128 MiB of HBM per device.

```python
import math
import jax
import jax.numpy as jnp
import numpy as np
from jax import lax

D = 960
QUERY_HEADS = 15
KEY_VALUE_HEADS = 5
HEAD_SIZE = 64
FF = 2560
TOK_DEV = 512
SEGS = 3
MOST = 384
QD = 960
KD = 320
ROWS = 32
TOKENS = 16384


def shard_levels(own_key, shape, pieces, least, largest):
    level = 1.0
    for dim, shards_of in pieces:
        heights = jax.random.uniform(jax.random.fold_in(jax.random.fold_in(own_key, 6), dim), (shards_of,), jnp.float32, least / len(pieces), largest / len(pieces))
        level = level * jnp.repeat(jnp.exp(heights), shape[dim] // shards_of).reshape((-1,) + (1,) * (len(shape) - 1 - dim))
    return level


def profile(amount, total, limit, slope):
    portions = [(1 << 20) // math.isqrt(standing ** slope) + 1 for standing in range(2, amount + 1)]
    rest, given = total - limit - (amount - 1), [1] * (amount - 1)
    while rest > 0:
        free = [i for i in range(amount - 1) if given[i] < limit]
        mass, remaining = sum([portions[i] for i in free]), rest
        for i in free:
            extra = min(limit - given[i], max(1, remaining * portions[i] // mass), rest)
            given[i] = given[i] + extra
            rest = rest - extra
    return np.array([limit] + given)


def uneven(key, count, total, reach, lean):
    if count == 2:
        one = jax.random.randint(key, (), max(1, total - reach), min(reach, total - 1) + 1)
        return jnp.stack([one, total - one])
    tallies = jnp.asarray(profile(count, total, reach, lean), jnp.int32)
    twos = (count - 1) // 2
    donor, sink = tallies[1:1 + 2 * twos:2], tallies[2:2 + 2 * twos:2]
    room = jnp.minimum(donor - 1, reach - sink)
    passed = jax.random.randint(jax.random.fold_in(key, 1), (twos,), 0, 1 << 20) % (room + 1)
    tallies = tallies.at[1:1 + 2 * twos:2].set(donor - passed).at[2:2 + 2 * twos:2].set(sink + passed)
    return tallies[jax.random.permutation(jax.random.fold_in(key, 2), count)]


def gaussian(own_key, extent, deviation, limit, split=(), kind=jnp.bfloat16):
    level = shard_levels(own_key, extent, split, -0.22, 0.18) if split else 1.0
    array = jax.random.normal(own_key, extent, jnp.float32) * deviation * level
    return jnp.minimum(jnp.maximum(array, -limit), limit).astype(kind)


def setup_inputs(seed: int = 0) -> dict:
    streams_of = jax.random.split(jax.random.key(seed), 13)
    layer_input = gaussian(streams_of[0], (TOKENS, D), 1.0, 6.0, ((0, 32),))
    segment_ids = jax.vmap(lambda own: jnp.searchsorted(jnp.cumsum(uneven(own, SEGS, TOK_DEV, MOST, 2)), jnp.arange(TOK_DEV), side="right"))(jax.random.split(streams_of[1], ROWS)).reshape((ROWS, TOK_DEV)).astype(jnp.int32)
    upstream_grad = gaussian(streams_of[2], (TOKENS, D), 1.0, 6.0, ((0, 32),))
    attn_gain = jnp.clip(1.0 + 0.1 * jax.random.normal(streams_of[3], (D,), jnp.float32), 0.5, 1.5).astype(jnp.bfloat16)
    query_weight = gaussian(streams_of[4], (D, QD), D ** -0.5, 0.1875, ((0, 2),))
    key_weight = gaussian(streams_of[5], (D, KD), D ** -0.5, 0.1875, ((0, 2),))
    value_weight = gaussian(streams_of[6], (D, KD), D ** -0.5, 0.1875, ((0, 2),))
    output_weight = gaussian(streams_of[7], (QD, D), (max(1, QD // 128)) ** -0.5, 2.0, ((0, 2),))
    ffn_gain = jnp.clip(1.0 + 0.1 * jax.random.normal(streams_of[8], (D,), jnp.float32), 0.5, 1.5).astype(jnp.bfloat16)
    gate_weight = gaussian(streams_of[9], (D, FF), D ** -0.5, 0.1875, ((1, 2),))
    up_weight = gaussian(streams_of[10], (D, FF), D ** -0.5, 0.1875, ((1, 2),))
    down_weight = gaussian(streams_of[11], (FF, D), FF ** -0.5, 0.125, ((0, 2),))
    return {"layer_input": layer_input, "segment_ids": segment_ids, "upstream_grad": upstream_grad, "attn_gain": attn_gain, "query_weight": query_weight, "key_weight": key_weight, "value_weight": value_weight, "output_weight": output_weight, "ffn_gain": ffn_gain, "gate_weight": gate_weight, "up_weight": up_weight, "down_weight": down_weight}


HIGH = lax.Precision.HIGHEST
EPSILON = 1e-05
NEGATIVE = -1e+30

@jax.custom_vjp
def low(v):
    return lax.optimization_barrier(v.astype(jnp.bfloat16)).astype(jnp.float32)

@jax.custom_vjp
def low_back(v):
    return v

def low_keep(v):
    return (low(v), None)

def low_pass(kept, grad):
    return (grad,)

def back_keep(v):
    return (v, None)

def back_low(kept, grad):
    return (low(grad),)
low.defvjp(low_keep, low_pass)
low_back.defvjp(back_keep, back_low)

def rms_norm(values, gain):
    return values * lax.rsqrt(lax.optimization_barrier(jnp.mean(values * values, -1, keepdims=True)) + EPSILON) * gain

def positions_of(segment):
    labels = jnp.arange(SEGS, dtype=jnp.int32)
    onehot = (segment[:, None] == labels[None, :]).astype(jnp.int32)
    counts = lax.optimization_barrier(jnp.sum(onehot, 0))
    starts = jnp.cumsum(counts) - counts
    first_index = lax.optimization_barrier(jnp.sum(onehot * starts[None, :], 1)).astype(jnp.int32)
    return jnp.arange(segment.shape[0], dtype=jnp.int32) - first_index

def rope_tables(segment):
    position = positions_of(segment).astype(jnp.float32)
    half_size = HEAD_SIZE // 2
    frequency = 10000.0 ** (-jnp.arange(half_size, dtype=jnp.float32) * 2.0 / HEAD_SIZE)
    angle = position[:, None] * frequency[None, :]
    cosine = jnp.concatenate([jnp.cos(angle), jnp.cos(angle)], 1)
    sine = jnp.concatenate([-jnp.sin(angle), jnp.sin(angle)], 1)
    return (cosine, sine)

def rotate(values, cosine, sine, sign):
    token_stack = values.shape[0]
    heads = values.shape[1] // HEAD_SIZE
    shaped = values.reshape(token_stack, heads, 2, HEAD_SIZE // 2)
    swapped = shaped[:, :, ::-1, :].reshape(token_stack, heads, HEAD_SIZE)
    plain = values.reshape(token_stack, heads, HEAD_SIZE)
    return (plain * cosine[:, None, :] + sign * swapped * sine[:, None, :]).reshape(token_stack, heads * HEAD_SIZE)

def layer_rows(hidden_in, segment, gain_one, query_w, key_w, value_w, output_w, gain_two, gate_w, up_w, down_w):
    token_stack = hidden_in.shape[0]
    shard_groups = QUERY_HEADS // KEY_VALUE_HEADS
    scale = HEAD_SIZE ** (-0.5)
    normed = low(rms_norm(hidden_in, gain_one))
    query_input = low_back(jnp.dot(normed, query_w, precision=HIGH))
    key_tensor = low_back(jnp.dot(normed, key_w, precision=HIGH))
    value_tensor = low(low_back(jnp.dot(normed, value_w, precision=HIGH)))
    cosine, sine = rope_tables(segment)
    query_input = low(rotate(query_input, cosine, sine, 1.0))
    key_tensor = low(rotate(key_tensor, cosine, sine, 1.0))
    index = jnp.arange(token_stack, dtype=jnp.int32)
    allowed = (index[None, :] <= index[:, None]) & (segment[None, :] == segment[:, None])
    heads_of_query = query_input.reshape(token_stack, KEY_VALUE_HEADS, shard_groups, HEAD_SIZE).transpose(1, 2, 0, 3)
    heads_of_key = key_tensor.reshape(token_stack, KEY_VALUE_HEADS, HEAD_SIZE).transpose(1, 0, 2)
    heads_of_value = value_tensor.reshape(token_stack, KEY_VALUE_HEADS, HEAD_SIZE).transpose(1, 0, 2)

    def one_head(operands):
        query_head, key_head, value_head = operands
        scores = low_back(scale * jnp.einsum('gqd,kd->gqk', query_head, key_head, precision=HIGH))
        scores = jnp.where(allowed[None], scores, NEGATIVE)
        shifted = scores - lax.optimization_barrier(jnp.max(scores, -1, keepdims=True))
        expo = jnp.exp(shifted)
        probs = low(expo / lax.optimization_barrier(jnp.sum(expo, -1, keepdims=True)))
        return jnp.einsum('gqk,kd->gqd', probs, value_head, precision=HIGH)
    heads_out = lax.map(jax.checkpoint(one_head), (heads_of_query, heads_of_key, heads_of_value))
    mixed = low(low_back(heads_out.transpose(2, 0, 1, 3).reshape(token_stack, QUERY_HEADS * HEAD_SIZE)))
    attended = low_back(jnp.dot(mixed, output_w, precision=HIGH))
    middle = hidden_in + attended
    normed_two = low(rms_norm(middle, gain_two))
    gate_value = low_back(jnp.dot(normed_two, gate_w, precision=HIGH))
    up_value = low_back(jnp.dot(normed_two, up_w, precision=HIGH))
    activ = low(gate_value * jax.nn.sigmoid(gate_value) * up_value)
    return middle + low_back(jnp.dot(activ, down_w, precision=HIGH))

def reference(layer_input, segment_ids, upstream_grad, attn_gain, query_weight, key_weight, value_weight, output_weight, ffn_gain, gate_weight, up_weight, down_weight):
    weights = tuple((w.astype(jnp.float32) for w in (attn_gain, query_weight, key_weight, value_weight, output_weight, ffn_gain, gate_weight, up_weight, down_weight)))
    start_input = layer_input.astype(jnp.float32)

    def forward(hidden_all, weight_set):
        row_blocks = hidden_all.reshape(-1, TOK_DEV, D)

        def one_row(operands):
            row_values, row_segments = operands
            return layer_rows(row_values, row_segments, *weight_set)
        result = lax.map(jax.checkpoint(one_row), (row_blocks, segment_ids))
        return result.reshape(-1, D)
    output_value, pullback = jax.vjp(forward, start_input, weights)
    grad_input, grad_weights = pullback(upstream_grad.astype(jnp.float32))
    return (output_value.astype(jnp.bfloat16), grad_input, grad_weights[0], grad_weights[1], grad_weights[2], grad_weights[3], grad_weights[4], grad_weights[5], grad_weights[6], grad_weights[7], grad_weights[8])
```

```python
import functools

import jax
import jax.numpy as jnp
from jax import lax
from jax.experimental import pallas as pl
from jax.experimental.pallas import tpu as pltpu
from jax.sharding import PartitionSpec as P

QUERY_HEADS = 15
KEY_VALUE_HEADS = 5
HEAD_SIZE = 64
SEGS = 3


EPSILON = 1e-05
NEGATIVE = -1e30


def product(left, right):
    return jnp.dot(left, right, preferred_element_type=jnp.float32)


def left_inner(left, right):
    return lax.dot_general(
        left, right, (((0,), (0,)), ((), ())), preferred_element_type=jnp.float32
    )


def right_inner(left, right):
    return lax.dot_general(
        left, right, (((1,), (1,)), ((), ())), preferred_element_type=jnp.float32
    )


def normalize(values):
    inverse = lax.rsqrt(jnp.mean(values * values, -1, keepdims=True) + EPSILON)
    return (values * inverse, inverse)


def norm_backward(grad_norm, normed, inverse):
    return inverse * (grad_norm - normed * jnp.mean(grad_norm * normed, -1, keepdims=True))


def positions_of(segment):
    labels = jnp.arange(SEGS, dtype=jnp.int32)
    onehot = (segment[:, None] == labels[None, :]).astype(jnp.int32)
    counts = jnp.sum(onehot, 0)
    starts = jnp.cumsum(counts) - counts
    first_index = jnp.sum(onehot * starts[None, :], 1)
    return jnp.arange(segment.shape[0], dtype=jnp.int32) - first_index


GROUP = QUERY_HEADS // KEY_VALUE_HEADS
SCALE = HEAD_SIZE ** (-0.5)


def contract(left, right, left_dim, right_dim):
    return lax.dot_general(
        left,
        right,
        (((left_dim,), (right_dim,)), ((), ())),
        preferred_element_type=jnp.float32,
    )


def rope_tables(segment):
    position = positions_of(segment).astype(jnp.float32)
    half_size = HEAD_SIZE // 2
    frequency = 10000.0 ** (-jnp.arange(half_size, dtype=jnp.float32) * 2.0 / HEAD_SIZE)
    angle = frequency[:, None] * position[None, :]
    return (jnp.cos(angle), jnp.sin(angle))


def rotate(values, cosine, sine):
    features, tokens = values.shape
    shaped = values.reshape(features // HEAD_SIZE, 2, HEAD_SIZE // 2, tokens)
    first, second = shaped[:, 0], shaped[:, 1]
    turned = jnp.stack(
        [first * cosine - second * sine, second * cosine + first * sine], 1
    )
    return turned.reshape(features, tokens)


def row_blocks(tokens):
    if tokens % 256 == 0:
        return [(start, 256, start + 256) for start in range(0, tokens, 256)]
    return [(0, tokens, tokens)]


def masked_probs(key_rows, query_columns, seg_col, seg_row, start):
    scores = contract(key_rows, query_columns, 1, 0) * SCALE
    key_index = lax.broadcasted_iota(jnp.int32, scores.shape, 0)
    query_index = lax.broadcasted_iota(jnp.int32, scores.shape, 1) + start
    allowed = (key_index <= query_index) & (seg_col == seg_row)
    scores = jnp.where(allowed, scores, NEGATIVE)
    expo = jnp.exp(scores - jnp.max(scores, 0, keepdims=True))
    return expo * (1.0 / jnp.sum(expo, 0, keepdims=True))


def forward_kernel(seg_col, seg_row, query, key_rows, value, out):
    tokens = query.shape[1]
    for start, count, keys in row_blocks(tokens):
        for member in range(GROUP):
            rows = slice(member * HEAD_SIZE, (member + 1) * HEAD_SIZE)
            columns = slice(start, start + count)
            probs = masked_probs(
                key_rows[0, :keys, :],
                query[rows, columns],
                seg_col[:keys, :],
                seg_row[:, columns],
                start,
            ).astype(jnp.bfloat16)
            out[rows, columns] = contract(value[:, :keys], probs, 1, 0).astype(jnp.bfloat16)


def backward_kernel(
    seg_col, seg_row, query, key, key_rows, value_rows, grad, query_out, key_out, value_out
):
    tokens = query.shape[1]
    key_out[...] = jnp.zeros_like(key_out)
    value_out[...] = jnp.zeros_like(value_out)
    for start, count, keys in row_blocks(tokens):
        for member in range(GROUP):
            rows = slice(member * HEAD_SIZE, (member + 1) * HEAD_SIZE)
            columns = slice(start, start + count)
            query_head = query[rows, columns]
            grad_head = grad[rows, columns]
            probs = masked_probs(
                key_rows[0, :keys, :], query_head, seg_col[:keys, :], seg_row[:, columns], start
            )
            grad_probs = contract(value_rows[0, :keys, :], grad_head, 1, 0)
            centre = jnp.sum(probs * grad_probs, 0, keepdims=True)
            grad_scores = (probs * (grad_probs - centre)).astype(jnp.bfloat16)
            query_out[rows, columns] = contract(key[:, :keys], grad_scores, 1, 0) * SCALE
            key_out[:, :keys] += contract(query_head, grad_scores, 1, 1) * SCALE
            value_out[:, :keys] += contract(grad_head, probs.astype(jnp.bfloat16), 1, 1)


def head_specs(tokens):
    group = pl.BlockSpec((GROUP * HEAD_SIZE, tokens), lambda j: (j, 0))
    single = pl.BlockSpec((HEAD_SIZE, tokens), lambda j: (j, 0))
    rows = pl.BlockSpec((1, tokens, HEAD_SIZE), lambda j: (j, 0, 0))
    seg_col = pl.BlockSpec((tokens, 1), lambda j: (0, 0))
    seg_row = pl.BlockSpec((1, tokens), lambda j: (0, 0))
    return group, single, rows, seg_col, seg_row


def attention_forward(segment, query, key_rows, value):
    tokens = query.shape[1]
    group, single, rows, seg_col, seg_row = head_specs(tokens)
    work = QUERY_HEADS * tokens * tokens
    return pl.pallas_call(
        forward_kernel,
        grid=(KEY_VALUE_HEADS,),
        out_shape=jax.ShapeDtypeStruct(query.shape, jnp.bfloat16),
        in_specs=[seg_col, seg_row, group, rows, single],
        out_specs=group,
        compiler_params=pltpu.CompilerParams(vmem_limit_bytes=40 * 2**20),
        cost_estimate=pl.CostEstimate(
            flops=work * HEAD_SIZE * 16, bytes_accessed=3 * 2**20, transcendentals=work
        ),
    )(segment[:, None], segment[None, :], query, key_rows, value)


def attention_backward(segment, query, key, key_rows, value_rows, grad):
    tokens = query.shape[1]
    group, single, rows, seg_col, seg_row = head_specs(tokens)
    work = QUERY_HEADS * tokens * tokens
    return pl.pallas_call(
        backward_kernel,
        grid=(KEY_VALUE_HEADS,),
        out_shape=(
            jax.ShapeDtypeStruct(query.shape, jnp.float32),
            jax.ShapeDtypeStruct(key.shape, jnp.float32),
            jax.ShapeDtypeStruct(key.shape, jnp.float32),
        ),
        in_specs=[seg_col, seg_row, group, single, rows, rows, group],
        out_specs=(group, single, single),
        compiler_params=pltpu.CompilerParams(vmem_limit_bytes=40 * 2**20),
        cost_estimate=pl.CostEstimate(
            flops=work * HEAD_SIZE * 40, bytes_accessed=8 * 2**20, transcendentals=work
        ),
    )(segment[:, None], segment[None, :], query, key, key_rows, value_rows, grad)


def by_rows(values):
    return values.reshape(-1, HEAD_SIZE, values.shape[1]).transpose(0, 2, 1)


def halving_dim(shape):
    if shape[0] % 16 == 0:
        return 0
    if shape[1] % 256 == 0:
        return 1
    return 0 if shape[0] % 2 == 0 else 1


def piece(values, which, dim, size):
    return lax.dynamic_slice_in_dim(values, which * size, size, dim)


def replica_sum(values, order, replicas):
    levels = replicas.bit_length() - 1
    if replicas != 1 << levels:
        return lax.psum(values, "replica").astype(jnp.float32)
    bits = [bit for bit in order if bit < levels]
    bits += [bit for bit in range(levels) if bit not in bits]
    index = lax.axis_index("replica")
    taken = []
    for bit in bits:
        pairs = [(i, i ^ (1 << bit)) for i in range(replicas)]
        dim = halving_dim(values.shape)
        size = values.shape[dim] // 2
        side = (index >> bit) & 1
        arrived = lax.ppermute(piece(values, 1 - side, dim, size), "replica", pairs)
        values = piece(values, side, dim, size) + arrived
        taken.append((pairs, dim, side))
    for pairs, dim, side in reversed(taken):
        arrived = lax.ppermute(values, "replica", pairs)
        low_side = side == 0
        values = jnp.concatenate(
            [jnp.where(low_side, values, arrived), jnp.where(low_side, arrived, values)], dim
        )
    return values.astype(jnp.float32)


def shard_sum(make, dim, full, shards):
    if shards == 2:
        size = full // 2
        side = lax.axis_index("shard")
        sent = make(1 - side, size).astype(jnp.bfloat16)
        arrived = lax.ppermute(sent, "shard", [(0, 1), (1, 0)])
        return (make(side, size) + arrived.astype(jnp.float32)).astype(jnp.bfloat16)
    whole = make(0, full).astype(jnp.bfloat16)
    return lax.psum_scatter(whole, "shard", scatter_dimension=dim, tiled=True)


def per_device(
    replicas,
    shards,
    layer_input,
    segment_ids,
    upstream_grad,
    attn_gain,
    query_weight,
    key_weight,
    value_weight,
    output_weight,
    ffn_gain,
    gate_weight,
    up_weight,
    down_weight,
):
    segment = segment_ids.reshape(-1)
    features = layer_input.shape[1]
    hidden = gate_weight.shape[1] * shards
    query_size, key_size = query_weight.shape[1], key_weight.shape[1]
    gains = lax.all_gather(jnp.stack([attn_gain, ffn_gain]), "shard", axis=1, tiled=True)
    projections = lax.all_gather(
        jnp.concatenate([query_weight, key_weight, value_weight], 1), "shard", axis=0, tiled=True
    )
    output_w = lax.all_gather(output_weight, "shard", axis=0, tiled=True)
    gate_w = lax.all_gather(gate_weight, "shard", axis=1, tiled=True)
    up_w = lax.all_gather(up_weight, "shard", axis=1, tiled=True)
    down_w = lax.all_gather(down_weight, "shard", axis=0, tiled=True)

    gain_one = gains[0].astype(jnp.float32)
    gain_two = gains[1].astype(jnp.float32)
    start_input = layer_input.astype(jnp.float32)
    normed_one, inverse_one = normalize(start_input)
    hidden_one = (normed_one * gain_one).astype(jnp.bfloat16)
    projected = contract(projections, hidden_one, 0, 1)
    cosine, sine = rope_tables(segment)
    turned = rotate(projected[: query_size + key_size], cosine, sine).astype(jnp.bfloat16)
    query, key = turned[:query_size], turned[query_size:]
    value = projected[query_size + key_size :].astype(jnp.bfloat16)
    key_rows, value_rows = by_rows(key), by_rows(value)
    mixed = attention_forward(segment, query, key_rows, value)
    middle = start_input + contract(mixed, output_w, 0, 0)
    normed_two, inverse_two = normalize(middle)
    hidden_two = (normed_two * gain_two).astype(jnp.bfloat16)

    gate_value = product(hidden_two, gate_w)
    up_value = product(hidden_two, up_w)
    sigma = jax.nn.sigmoid(gate_value)
    grad_activ = right_inner(upstream_grad, down_w)
    activ_low = (gate_value * sigma * up_value).astype(jnp.bfloat16)
    grad_gate = (grad_activ * up_value * sigma * (1.0 + gate_value * (1.0 - sigma))).astype(
        jnp.bfloat16
    )
    grad_up = (grad_activ * gate_value * sigma).astype(jnp.bfloat16)

    gate_grad = shard_sum(
        lambda which, size: left_inner(hidden_two, piece(grad_gate, which, 1, size)),
        1,
        hidden,
        shards,
    )
    gate_grad = replica_sum(gate_grad, ORDERS[0], replicas)
    up_grad = shard_sum(
        lambda which, size: left_inner(hidden_two, piece(grad_up, which, 1, size)),
        1,
        hidden,
        shards,
    )
    up_grad = replica_sum(up_grad, ORDERS[1], replicas)
    down_grad = shard_sum(
        lambda which, size: left_inner(piece(activ_low, which, 1, size), upstream_grad),
        0,
        hidden,
        shards,
    )
    down_grad = replica_sum(down_grad, ORDERS[2], replicas)

    layer_output = (middle + product(activ_low, down_w)).astype(jnp.bfloat16)
    grad_hidden_two = right_inner(grad_gate, gate_w) + right_inner(grad_up, up_w)
    gain_two_part = jnp.sum(grad_hidden_two * normed_two, 0)
    grad_middle = upstream_grad.astype(jnp.float32) + norm_backward(
        grad_hidden_two * gain_two, normed_two, inverse_two
    )
    grad_middle_low = grad_middle.astype(jnp.bfloat16)

    rows = features // shards
    padded = -(-(rows + 1) // 128) * 128

    output_part = contract(mixed, grad_middle_low, 1, 0)
    output_grad = shard_sum(
        lambda which, size: piece(output_part, which, 0, size), 0, query_size, shards
    )
    output_grad = jnp.pad(output_grad, ((0, padded - output_grad.shape[0]), (0, 0)))
    output_grad = replica_sum(output_grad, ORDERS[2], replicas)[: query_size // shards]

    grad_mixed = contract(output_w, grad_middle_low, 1, 1).astype(jnp.bfloat16)
    grad_query, grad_key, grad_value = attention_backward(
        segment, query, key, key_rows, value_rows, grad_mixed
    )
    grad_projected = jnp.concatenate(
        [
            rotate(grad_query, cosine, -sine).astype(jnp.bfloat16),
            rotate(grad_key, cosine, -sine).astype(jnp.bfloat16),
            grad_value.astype(jnp.bfloat16),
        ],
        0,
    )
    grad_hidden_one = contract(grad_projected, projections, 0, 1)
    gain_one_part = jnp.sum(grad_hidden_one * normed_one, 0)
    input_grad = grad_middle + norm_backward(grad_hidden_one * gain_one, normed_one, inverse_one)

    projection_part = contract(hidden_one, grad_projected, 0, 1)
    width = projection_part.shape[1]
    gain_parts = jnp.stack([gain_one_part, gain_two_part]).reshape(2, shards, rows)
    gain_rows = gain_parts.transpose(1, 0, 2).reshape(shards, 1, 2 * rows)
    gain_rows = jnp.pad(gain_rows, ((0, 0), (0, padded - rows - 1), (0, width - 2 * rows)))
    packed = jnp.concatenate([projection_part.reshape(shards, rows, width), gain_rows], 1)
    packed = packed.reshape(shards * padded, width)
    packed = shard_sum(
        lambda which, size: piece(packed, which, 0, size), 0, shards * padded, shards
    )
    cuts = [0, width // 384 * 128, width // 384 * 256, width]
    packed = jnp.concatenate(
        [
            replica_sum(packed[:, cuts[i] : cuts[i + 1]], ORDERS[i], replicas)
            for i in range(3)
        ],
        1,
    )
    query_grad = packed[:rows, :query_size]
    key_grad = packed[:rows, query_size : query_size + key_size]
    value_grad = packed[:rows, query_size + key_size :]
    gain_one_grad = packed[rows, :rows]
    gain_two_grad = packed[rows, rows : 2 * rows]
    return (
        layer_output,
        input_grad,
        gain_one_grad,
        query_grad,
        key_grad,
        value_grad,
        output_grad,
        gain_two_grad,
        gate_grad,
        up_grad,
        down_grad,
    )


ORDERS = ((0, 1, 2, 3), (1, 2, 0, 3), (2, 0, 1, 3))


def solution(mesh):
    placed = (
        P(("replica", "shard"), None),
        P(("replica", "shard"), None),
        P(("replica", "shard"), None),
        P("shard"),
        P("shard", None),
        P("shard", None),
        P("shard", None),
        P("shard", None),
        P("shard"),
        P(None, "shard"),
        P(None, "shard"),
        P("shard", None),
    )
    return jax.shard_map(
        functools.partial(per_device, mesh.shape["replica"], mesh.shape["shard"]),
        mesh=mesh,
        in_specs=placed,
        out_specs=(
            P(("replica", "shard"), None),
            P(("replica", "shard"), None),
            P("shard"),
            P("shard", None),
            P("shard", None),
            P("shard", None),
            P("shard", None),
            P("shard"),
            P(None, "shard"),
            P(None, "shard"),
            P("shard", None),
        ),
        check_vma=False,
    )
```

```python
import functools

import jax
import jax.numpy as jnp
from jax import lax
from jax.experimental import pallas as pl
from jax.experimental.pallas import tpu as pltpu
from jax.sharding import PartitionSpec as P

QUERY_HEADS = 15
KEY_VALUE_HEADS = 5
HEAD_SIZE = 64
SEGS = 3


EPSILON = 1e-05
NEGATIVE = -1e30


def product(left, right):
    return jnp.dot(left, right, preferred_element_type=jnp.float32)


def left_inner(left, right):
    return lax.dot_general(
        left, right, (((0,), (0,)), ((), ())), preferred_element_type=jnp.float32
    )


def right_inner(left, right):
    return lax.dot_general(
        left, right, (((1,), (1,)), ((), ())), preferred_element_type=jnp.float32
    )


def normalize(values):
    inverse = lax.rsqrt(jnp.mean(values * values, -1, keepdims=True) + EPSILON)
    return (values * inverse, inverse)


def norm_backward(grad_norm, normed, inverse):
    return inverse * (grad_norm - normed * jnp.mean(grad_norm * normed, -1, keepdims=True))


def positions_of(segment):
    labels = jnp.arange(SEGS, dtype=jnp.int32)
    onehot = (segment[:, None] == labels[None, :]).astype(jnp.int32)
    counts = jnp.sum(onehot, 0)
    starts = jnp.cumsum(counts) - counts
    first_index = jnp.sum(onehot * starts[None, :], 1)
    return jnp.arange(segment.shape[0], dtype=jnp.int32) - first_index


GROUP = QUERY_HEADS // KEY_VALUE_HEADS
SCALE = HEAD_SIZE ** (-0.5)


def contract(left, right, left_dim, right_dim):
    return lax.dot_general(
        left,
        right,
        (((left_dim,), (right_dim,)), ((), ())),
        preferred_element_type=jnp.float32,
    )


def rope_tables(segment):
    position = positions_of(segment).astype(jnp.float32)
    half_size = HEAD_SIZE // 2
    frequency = 10000.0 ** (-jnp.arange(half_size, dtype=jnp.float32) * 2.0 / HEAD_SIZE)
    angle = frequency[:, None] * position[None, :]
    return (jnp.cos(angle), jnp.sin(angle))


def rotate(values, cosine, sine):
    features, tokens = values.shape
    shaped = values.reshape(features // HEAD_SIZE, 2, HEAD_SIZE // 2, tokens)
    first, second = shaped[:, 0], shaped[:, 1]
    turned = jnp.stack(
        [first * cosine - second * sine, second * cosine + first * sine], 1
    )
    return turned.reshape(features, tokens)


def row_blocks(tokens):
    if tokens % 256 == 0:
        return [(start, 256, start + 256) for start in range(0, tokens, 256)]
    return [(0, tokens, tokens)]


def masked_probs(key_rows, query_columns, seg_col, seg_row, start):
    scores = contract(key_rows, query_columns, 1, 0) * SCALE
    key_index = lax.broadcasted_iota(jnp.int32, scores.shape, 0)
    query_index = lax.broadcasted_iota(jnp.int32, scores.shape, 1) + start
    allowed = (key_index <= query_index) & (seg_col == seg_row)
    scores = jnp.where(allowed, scores, NEGATIVE)
    expo = jnp.exp(scores - jnp.max(scores, 0, keepdims=True))
    return expo * (1.0 / jnp.sum(expo, 0, keepdims=True))


def forward_kernel(seg_col, seg_row, query, key_rows, value, out):
    tokens = query.shape[1]
    for start, count, keys in row_blocks(tokens):
        for member in range(GROUP):
            rows = slice(member * HEAD_SIZE, (member + 1) * HEAD_SIZE)
            columns = slice(start, start + count)
            probs = masked_probs(
                key_rows[0, :keys, :],
                query[rows, columns],
                seg_col[:keys, :],
                seg_row[:, columns],
                start,
            ).astype(jnp.bfloat16)
            out[rows, columns] = contract(value[:, :keys], probs, 1, 0).astype(jnp.bfloat16)


def backward_kernel(
    seg_col, seg_row, query, key, key_rows, value_rows, grad, query_out, key_out, value_out
):
    tokens = query.shape[1]
    key_out[...] = jnp.zeros_like(key_out)
    value_out[...] = jnp.zeros_like(value_out)
    for start, count, keys in row_blocks(tokens):
        for member in range(GROUP):
            rows = slice(member * HEAD_SIZE, (member + 1) * HEAD_SIZE)
            columns = slice(start, start + count)
            query_head = query[rows, columns]
            grad_head = grad[rows, columns]
            probs = masked_probs(
                key_rows[0, :keys, :], query_head, seg_col[:keys, :], seg_row[:, columns], start
            )
            grad_probs = contract(value_rows[0, :keys, :], grad_head, 1, 0)
            centre = jnp.sum(probs * grad_probs, 0, keepdims=True)
            grad_scores = (probs * (grad_probs - centre)).astype(jnp.bfloat16)
            query_out[rows, columns] = contract(key[:, :keys], grad_scores, 1, 0) * SCALE
            key_out[:, :keys] += contract(query_head, grad_scores, 1, 1) * SCALE
            value_out[:, :keys] += contract(grad_head, probs.astype(jnp.bfloat16), 1, 1)


def head_specs(tokens):
    group = pl.BlockSpec((GROUP * HEAD_SIZE, tokens), lambda j: (j, 0))
    single = pl.BlockSpec((HEAD_SIZE, tokens), lambda j: (j, 0))
    rows = pl.BlockSpec((1, tokens, HEAD_SIZE), lambda j: (j, 0, 0))
    seg_col = pl.BlockSpec((tokens, 1), lambda j: (0, 0))
    seg_row = pl.BlockSpec((1, tokens), lambda j: (0, 0))
    return group, single, rows, seg_col, seg_row


def attention_forward(segment, query, key_rows, value):
    tokens = query.shape[1]
    group, single, rows, seg_col, seg_row = head_specs(tokens)
    work = QUERY_HEADS * tokens * tokens
    return pl.pallas_call(
        forward_kernel,
        grid=(KEY_VALUE_HEADS,),
        out_shape=jax.ShapeDtypeStruct(query.shape, jnp.bfloat16),
        in_specs=[seg_col, seg_row, group, rows, single],
        out_specs=group,
        compiler_params=pltpu.CompilerParams(vmem_limit_bytes=40 * 2**20),
        cost_estimate=pl.CostEstimate(
            flops=work * HEAD_SIZE * 16, bytes_accessed=3 * 2**20, transcendentals=work
        ),
    )(segment[:, None], segment[None, :], query, key_rows, value)


def attention_backward(segment, query, key, key_rows, value_rows, grad):
    tokens = query.shape[1]
    group, single, rows, seg_col, seg_row = head_specs(tokens)
    work = QUERY_HEADS * tokens * tokens
    return pl.pallas_call(
        backward_kernel,
        grid=(KEY_VALUE_HEADS,),
        out_shape=(
            jax.ShapeDtypeStruct(query.shape, jnp.float32),
            jax.ShapeDtypeStruct(key.shape, jnp.float32),
            jax.ShapeDtypeStruct(key.shape, jnp.float32),
        ),
        in_specs=[seg_col, seg_row, group, single, rows, rows, group],
        out_specs=(group, single, single),
        compiler_params=pltpu.CompilerParams(vmem_limit_bytes=40 * 2**20),
        cost_estimate=pl.CostEstimate(
            flops=work * HEAD_SIZE * 40, bytes_accessed=8 * 2**20, transcendentals=work
        ),
    )(segment[:, None], segment[None, :], query, key, key_rows, value_rows, grad)


def by_rows(values):
    return values.reshape(-1, HEAD_SIZE, values.shape[1]).transpose(0, 2, 1)


def gather_rows(values, shards):
    if shards != 2:
        return lax.all_gather(values, "shard", axis=0, tiled=True)
    arrived = lax.ppermute(values, "shard", [(0, 1), (1, 0)])
    first = lax.axis_index("shard") == 0
    return jnp.concatenate(
        [jnp.where(first, values, arrived), jnp.where(first, arrived, values)], 0
    )


def others(values, shards):
    blocks = [values]
    for step in range(1, shards):
        pairs = [((i + step) % shards, i) for i in range(shards)]
        blocks.append(lax.ppermute(values, "shard", pairs))
    return blocks


def returned(parts, shards):
    total = parts[0]
    for step in range(1, shards):
        pairs = [(i, (i + step) % shards) for i in range(shards)]
        total = total + lax.ppermute(parts[step].astype(jnp.bfloat16), "shard", pairs).astype(
            jnp.float32
        )
    return total.astype(jnp.bfloat16)


def per_device(
    shards,
    layer_input,
    segment_ids,
    upstream_grad,
    attn_gain,
    query_weight,
    key_weight,
    value_weight,
    output_weight,
    ffn_gain,
    gate_weight,
    up_weight,
    down_weight,
):
    segment = segment_ids.reshape(-1)
    features = layer_input.shape[1]
    query_size, key_size = query_weight.shape[1], key_weight.shape[1]
    gains = gather_rows(jnp.stack([attn_gain, ffn_gain], 1), shards)
    projections = gather_rows(
        jnp.concatenate([query_weight, key_weight, value_weight], 1), shards
    )
    output_w = gather_rows(output_weight, shards)
    gate_blocks = others(gate_weight, shards)
    up_blocks = others(up_weight, shards)
    down_blocks = others(down_weight, shards)

    gain_one = gains[:, 0].astype(jnp.float32)
    gain_two = gains[:, 1].astype(jnp.float32)
    start_input = layer_input.astype(jnp.float32)
    normed_one, inverse_one = normalize(start_input)
    hidden_one = (normed_one * gain_one).astype(jnp.bfloat16)
    projected = contract(projections, hidden_one, 0, 1)
    cosine, sine = rope_tables(segment)
    turned = rotate(projected[: query_size + key_size], cosine, sine).astype(jnp.bfloat16)
    query, key = turned[:query_size], turned[query_size:]
    value = projected[query_size + key_size :].astype(jnp.bfloat16)
    key_rows, value_rows = by_rows(key), by_rows(value)
    mixed = attention_forward(segment, query, key_rows, value)
    middle = start_input + contract(mixed, output_w, 0, 0)
    normed_two, inverse_two = normalize(middle)
    hidden_two = (normed_two * gain_two).astype(jnp.bfloat16)

    grad_hidden_two = jnp.zeros_like(middle)
    down_out = middle
    gate_parts, up_parts, down_parts = [], [], []
    for gate_w, up_w, down_w in zip(gate_blocks, up_blocks, down_blocks):
        gate_value = product(hidden_two, gate_w)
        up_value = product(hidden_two, up_w)
        sigma = jax.nn.sigmoid(gate_value)
        grad_activ = right_inner(upstream_grad, down_w)
        activ_low = (gate_value * sigma * up_value).astype(jnp.bfloat16)
        grad_gate = (grad_activ * up_value * sigma * (1.0 + gate_value * (1.0 - sigma))).astype(
            jnp.bfloat16
        )
        grad_up = (grad_activ * gate_value * sigma).astype(jnp.bfloat16)
        gate_parts.append(left_inner(hidden_two, grad_gate))
        up_parts.append(left_inner(hidden_two, grad_up))
        down_parts.append(left_inner(activ_low, upstream_grad))
        down_out = down_out + product(activ_low, down_w)
        grad_hidden_two = (
            grad_hidden_two + right_inner(grad_gate, gate_w) + right_inner(grad_up, up_w)
        )
    layer_output = down_out.astype(jnp.bfloat16)
    ffn_own = (
        returned(gate_parts, shards),
        returned(up_parts, shards),
        returned(down_parts, shards),
    )
    ffn_sums = lax.psum(ffn_own, "replica")
    gain_two_part = jnp.sum(grad_hidden_two * normed_two, 0)
    grad_middle = upstream_grad.astype(jnp.float32) + norm_backward(
        grad_hidden_two * gain_two, normed_two, inverse_two
    )
    grad_middle_low = grad_middle.astype(jnp.bfloat16)

    rows = features // shards
    padded = -(-(rows + 1) // 16) * 16

    output_part = contract(mixed, grad_middle_low, 1, 0)
    grad_mixed = contract(output_w, grad_middle_low, 1, 1).astype(jnp.bfloat16)
    grad_mixed, _ = lax.optimization_barrier((grad_mixed, ffn_own))
    grad_query, grad_key, grad_value = attention_backward(
        segment, query, key, key_rows, value_rows, grad_mixed
    )
    grad_projected = jnp.concatenate(
        [
            rotate(grad_query, cosine, -sine).astype(jnp.bfloat16),
            rotate(grad_key, cosine, -sine).astype(jnp.bfloat16),
            grad_value.astype(jnp.bfloat16),
        ],
        0,
    )
    grad_hidden_one = contract(grad_projected, projections, 0, 1)
    gain_one_part = jnp.sum(grad_hidden_one * normed_one, 0)
    input_grad = grad_middle + norm_backward(grad_hidden_one * gain_one, normed_one, inverse_one)

    projection_part = jnp.concatenate(
        [contract(hidden_one, grad_projected, 0, 1), output_part], 1
    ).astype(jnp.bfloat16)
    width = projection_part.shape[1]
    gain_parts = jnp.stack([gain_one_part, gain_two_part]).reshape(2, shards, rows)
    gain_rows = gain_parts.transpose(1, 0, 2).reshape(shards, 1, 2 * rows)
    gain_rows = jnp.pad(gain_rows, ((0, 0), (0, padded - rows - 1), (0, width - 2 * rows)))
    packed = jnp.concatenate(
        [projection_part.reshape(shards, rows, width), gain_rows.astype(jnp.bfloat16)], 1
    )
    side = lax.axis_index("shard")
    packed = [
        lax.dynamic_index_in_dim(packed, lax.rem(side + step, shards), 0, keepdims=False).astype(
            jnp.float32
        )
        for step in range(shards)
    ]
    packed, ffn_sums = lax.optimization_barrier((returned(packed, shards), ffn_sums))
    packed = lax.psum(packed, "replica").astype(jnp.float32)
    gate_grad, up_grad, down_grad = [total.astype(jnp.float32) for total in ffn_sums]
    ends = [query_size, query_size + key_size, query_size + 2 * key_size]
    query_grad = packed[:rows, : ends[0]]
    key_grad = packed[:rows, ends[0] : ends[1]]
    value_grad = packed[:rows, ends[1] : ends[2]]
    output_grad = packed[:rows, ends[2] :]
    gain_one_grad = packed[rows, :rows]
    gain_two_grad = packed[rows, rows : 2 * rows]
    return (
        layer_output,
        input_grad,
        gain_one_grad,
        query_grad,
        key_grad,
        value_grad,
        output_grad,
        gain_two_grad,
        gate_grad,
        up_grad,
        down_grad,
    )


def solution(mesh):
    placed = (
        P(("replica", "shard"), None),
        P(("replica", "shard"), None),
        P(("replica", "shard"), None),
        P("shard"),
        P("shard", None),
        P("shard", None),
        P("shard", None),
        P("shard", None),
        P("shard"),
        P(None, "shard"),
        P(None, "shard"),
        P("shard", None),
    )
    return jax.shard_map(
        functools.partial(per_device, mesh.shape["shard"]),
        mesh=mesh,
        in_specs=placed,
        out_specs=(
            P(("replica", "shard"), None),
            P(("replica", "shard"), None),
            P("shard"),
            P("shard", None),
            P("shard", None),
            P("shard", None),
            P("shard", None),
            P("shard"),
            P(None, "shard"),
            P(None, "shard"),
            P("shard", None),
        ),
        check_vma=False,
    )
```

```python
import functools

import jax
import jax.numpy as jnp
from jax import lax
from jax.experimental import pallas as pl
from jax.experimental.pallas import tpu as pltpu
from jax.sharding import PartitionSpec as P

QUERY_HEADS = 15
KEY_VALUE_HEADS = 5
HEAD_SIZE = 64
SEGS = 3


EPSILON = 1e-05
NEGATIVE = -1e30


def product(left, right):
    return jnp.dot(left, right, preferred_element_type=jnp.float32)


def left_inner(left, right):
    return lax.dot_general(
        left, right, (((0,), (0,)), ((), ())), preferred_element_type=jnp.float32
    )


def right_inner(left, right):
    return lax.dot_general(
        left, right, (((1,), (1,)), ((), ())), preferred_element_type=jnp.float32
    )


def normalize(values):
    inverse = lax.rsqrt(jnp.mean(values * values, -1, keepdims=True) + EPSILON)
    return (values * inverse, inverse)


def norm_backward(grad_norm, normed, inverse):
    return inverse * (grad_norm - normed * jnp.mean(grad_norm * normed, -1, keepdims=True))


def positions_of(segment):
    labels = jnp.arange(SEGS, dtype=jnp.int32)
    onehot = (segment[:, None] == labels[None, :]).astype(jnp.int32)
    counts = jnp.sum(onehot, 0)
    starts = jnp.cumsum(counts) - counts
    first_index = jnp.sum(onehot * starts[None, :], 1)
    return jnp.arange(segment.shape[0], dtype=jnp.int32) - first_index


GROUP = QUERY_HEADS // KEY_VALUE_HEADS
SCALE = HEAD_SIZE ** (-0.5)


def contract(left, right, left_dim, right_dim):
    return lax.dot_general(
        left,
        right,
        (((left_dim,), (right_dim,)), ((), ())),
        preferred_element_type=jnp.float32,
    )


def rope_tables(segment):
    position = positions_of(segment).astype(jnp.float32)
    half_size = HEAD_SIZE // 2
    frequency = 10000.0 ** (-jnp.arange(half_size, dtype=jnp.float32) * 2.0 / HEAD_SIZE)
    angle = frequency[:, None] * position[None, :]
    return (jnp.cos(angle), jnp.sin(angle))


def rotate(values, cosine, sine):
    features, tokens = values.shape
    shaped = values.reshape(features // HEAD_SIZE, 2, HEAD_SIZE // 2, tokens)
    first, second = shaped[:, 0], shaped[:, 1]
    turned = jnp.stack(
        [first * cosine - second * sine, second * cosine + first * sine], 1
    )
    return turned.reshape(features, tokens)


def row_blocks(tokens):
    if tokens % 256 == 0:
        return [(start, 256, start + 256) for start in range(0, tokens, 256)]
    return [(0, tokens, tokens)]


def masked_probs(key_rows, query_columns, seg_col, seg_row, start):
    scores = contract(key_rows, query_columns, 1, 0) * SCALE
    key_index = lax.broadcasted_iota(jnp.int32, scores.shape, 0)
    query_index = lax.broadcasted_iota(jnp.int32, scores.shape, 1) + start
    allowed = (key_index <= query_index) & (seg_col == seg_row)
    scores = jnp.where(allowed, scores, NEGATIVE)
    expo = jnp.exp(scores - jnp.max(scores, 0, keepdims=True))
    return expo * (1.0 / jnp.sum(expo, 0, keepdims=True))


def forward_kernel(seg_col, seg_row, query, key_rows, value, out):
    tokens = query.shape[1]
    for start, count, keys in row_blocks(tokens):
        for member in range(GROUP):
            rows = slice(member * HEAD_SIZE, (member + 1) * HEAD_SIZE)
            columns = slice(start, start + count)
            probs = masked_probs(
                key_rows[0, :keys, :],
                query[rows, columns],
                seg_col[:keys, :],
                seg_row[:, columns],
                start,
            ).astype(jnp.bfloat16)
            out[rows, columns] = contract(value[:, :keys], probs, 1, 0).astype(jnp.bfloat16)


def backward_kernel(
    seg_col, seg_row, query, key, key_rows, value_rows, grad, query_out, key_out, value_out
):
    tokens = query.shape[1]
    key_out[...] = jnp.zeros_like(key_out)
    value_out[...] = jnp.zeros_like(value_out)
    for start, count, keys in row_blocks(tokens):
        for member in range(GROUP):
            rows = slice(member * HEAD_SIZE, (member + 1) * HEAD_SIZE)
            columns = slice(start, start + count)
            query_head = query[rows, columns]
            grad_head = grad[rows, columns]
            probs = masked_probs(
                key_rows[0, :keys, :], query_head, seg_col[:keys, :], seg_row[:, columns], start
            )
            grad_probs = contract(value_rows[0, :keys, :], grad_head, 1, 0)
            centre = jnp.sum(probs * grad_probs, 0, keepdims=True)
            grad_scores = (probs * (grad_probs - centre)).astype(jnp.bfloat16)
            query_out[rows, columns] = contract(key[:, :keys], grad_scores, 1, 0) * SCALE
            key_out[:, :keys] += contract(query_head, grad_scores, 1, 1) * SCALE
            value_out[:, :keys] += contract(grad_head, probs.astype(jnp.bfloat16), 1, 1)


def head_specs(tokens):
    group = pl.BlockSpec((GROUP * HEAD_SIZE, tokens), lambda j: (j, 0))
    single = pl.BlockSpec((HEAD_SIZE, tokens), lambda j: (j, 0))
    rows = pl.BlockSpec((1, tokens, HEAD_SIZE), lambda j: (j, 0, 0))
    seg_col = pl.BlockSpec((tokens, 1), lambda j: (0, 0))
    seg_row = pl.BlockSpec((1, tokens), lambda j: (0, 0))
    return group, single, rows, seg_col, seg_row


def attention_forward(segment, query, key_rows, value):
    tokens = query.shape[1]
    group, single, rows, seg_col, seg_row = head_specs(tokens)
    work = QUERY_HEADS * tokens * tokens
    return pl.pallas_call(
        forward_kernel,
        grid=(KEY_VALUE_HEADS,),
        out_shape=jax.ShapeDtypeStruct(query.shape, jnp.bfloat16),
        in_specs=[seg_col, seg_row, group, rows, single],
        out_specs=group,
        compiler_params=pltpu.CompilerParams(vmem_limit_bytes=40 * 2**20),
        cost_estimate=pl.CostEstimate(
            flops=work * HEAD_SIZE * 16, bytes_accessed=3 * 2**20, transcendentals=work
        ),
    )(segment[:, None], segment[None, :], query, key_rows, value)


def attention_backward(segment, query, key, key_rows, value_rows, grad):
    tokens = query.shape[1]
    group, single, rows, seg_col, seg_row = head_specs(tokens)
    work = QUERY_HEADS * tokens * tokens
    return pl.pallas_call(
        backward_kernel,
        grid=(KEY_VALUE_HEADS,),
        out_shape=(
            jax.ShapeDtypeStruct(query.shape, jnp.float32),
            jax.ShapeDtypeStruct(key.shape, jnp.float32),
            jax.ShapeDtypeStruct(key.shape, jnp.float32),
        ),
        in_specs=[seg_col, seg_row, group, single, rows, rows, group],
        out_specs=(group, single, single),
        compiler_params=pltpu.CompilerParams(vmem_limit_bytes=40 * 2**20),
        cost_estimate=pl.CostEstimate(
            flops=work * HEAD_SIZE * 40, bytes_accessed=8 * 2**20, transcendentals=work
        ),
    )(segment[:, None], segment[None, :], query, key, key_rows, value_rows, grad)


def by_rows(values):
    return values.reshape(-1, HEAD_SIZE, values.shape[1]).transpose(0, 2, 1)


def gather_rows(values, shards):
    if shards != 2:
        return lax.all_gather(values, "shard", axis=0, tiled=True)
    arrived = lax.ppermute(values, "shard", [(0, 1), (1, 0)])
    first = lax.axis_index("shard") == 0
    return jnp.concatenate(
        [jnp.where(first, values, arrived), jnp.where(first, arrived, values)], 0
    )


def others(values, shards):
    blocks = [values]
    for step in range(1, shards):
        pairs = [((i + step) % shards, i) for i in range(shards)]
        blocks.append(lax.ppermute(values, "shard", pairs))
    return blocks


def returned(parts, shards):
    total = parts[0]
    for step in range(1, shards):
        pairs = [(i, (i + step) % shards) for i in range(shards)]
        total = total + lax.ppermute(parts[step].astype(jnp.bfloat16), "shard", pairs).astype(
            jnp.float32
        )
    return total.astype(jnp.bfloat16)


def per_device(
    shards,
    layer_input,
    segment_ids,
    upstream_grad,
    attn_gain,
    query_weight,
    key_weight,
    value_weight,
    output_weight,
    ffn_gain,
    gate_weight,
    up_weight,
    down_weight,
):
    segment = segment_ids.reshape(-1)
    features = layer_input.shape[1]
    query_size, key_size = query_weight.shape[1], key_weight.shape[1]
    gains = gather_rows(jnp.stack([attn_gain, ffn_gain], 1), shards)
    projections = gather_rows(
        jnp.concatenate([query_weight, key_weight, value_weight], 1), shards
    )
    output_w = gather_rows(output_weight, shards)
    gate_blocks = others(gate_weight, shards)
    up_blocks = others(up_weight, shards)
    down_blocks = others(down_weight, shards)

    gain_one = gains[:, 0].astype(jnp.float32)
    gain_two = gains[:, 1].astype(jnp.float32)
    start_input = layer_input.astype(jnp.float32)
    normed_one, inverse_one = normalize(start_input)
    hidden_one = (normed_one * gain_one).astype(jnp.bfloat16)
    projected = contract(projections, hidden_one, 0, 1)
    cosine, sine = rope_tables(segment)
    turned = rotate(projected[: query_size + key_size], cosine, sine).astype(jnp.bfloat16)
    query, key = turned[:query_size], turned[query_size:]
    value = projected[query_size + key_size :].astype(jnp.bfloat16)
    key_rows, value_rows = by_rows(key), by_rows(value)
    mixed = attention_forward(segment, query, key_rows, value)
    middle = start_input + contract(mixed, output_w, 0, 0)
    normed_two, inverse_two = normalize(middle)
    hidden_two = (normed_two * gain_two).astype(jnp.bfloat16)

    grad_hidden_two = jnp.zeros_like(middle)
    down_out = middle
    gate_parts, up_parts, down_parts = [], [], []
    for gate_w, up_w, down_w in zip(gate_blocks, up_blocks, down_blocks):
        gate_value = product(hidden_two, gate_w)
        up_value = product(hidden_two, up_w)
        sigma = jax.nn.sigmoid(gate_value)
        grad_activ = right_inner(upstream_grad, down_w)
        activ_low = (gate_value * sigma * up_value).astype(jnp.bfloat16)
        grad_gate = (grad_activ * up_value * sigma * (1.0 + gate_value * (1.0 - sigma))).astype(
            jnp.bfloat16
        )
        grad_up = (grad_activ * gate_value * sigma).astype(jnp.bfloat16)
        gate_parts.append(left_inner(hidden_two, grad_gate))
        up_parts.append(left_inner(hidden_two, grad_up))
        down_parts.append(left_inner(activ_low, upstream_grad))
        down_out = down_out + product(activ_low, down_w)
        grad_hidden_two = (
            grad_hidden_two + right_inner(grad_gate, gate_w) + right_inner(grad_up, up_w)
        )
    layer_output = down_out.astype(jnp.bfloat16)
    ffn_own = (
        returned(gate_parts, shards),
        returned(up_parts, shards),
        returned(down_parts, shards),
    )
    gain_two_part = jnp.sum(grad_hidden_two * normed_two, 0)
    grad_middle = upstream_grad.astype(jnp.float32) + norm_backward(
        grad_hidden_two * gain_two, normed_two, inverse_two
    )
    grad_middle_low = grad_middle.astype(jnp.bfloat16)

    rows = features // shards
    padded = -(-(rows + 1) // 16) * 16

    output_part = contract(mixed, grad_middle_low, 1, 0)
    grad_mixed = contract(output_w, grad_middle_low, 1, 1).astype(jnp.bfloat16)
    grad_query, grad_key, grad_value = attention_backward(
        segment, query, key, key_rows, value_rows, grad_mixed
    )
    grad_projected = jnp.concatenate(
        [
            rotate(grad_query, cosine, -sine).astype(jnp.bfloat16),
            rotate(grad_key, cosine, -sine).astype(jnp.bfloat16),
            grad_value.astype(jnp.bfloat16),
        ],
        0,
    )
    grad_hidden_one = contract(grad_projected, projections, 0, 1)
    gain_one_part = jnp.sum(grad_hidden_one * normed_one, 0)
    input_grad = grad_middle + norm_backward(grad_hidden_one * gain_one, normed_one, inverse_one)

    projection_part = jnp.concatenate(
        [contract(hidden_one, grad_projected, 0, 1), output_part], 1
    ).astype(jnp.bfloat16)
    width = projection_part.shape[1]
    gain_parts = jnp.stack([gain_one_part, gain_two_part]).reshape(2, shards, rows)
    gain_rows = gain_parts.transpose(1, 0, 2).reshape(shards, 1, 2 * rows)
    gain_rows = jnp.pad(gain_rows, ((0, 0), (0, padded - rows - 1), (0, width - 2 * rows)))
    packed = jnp.concatenate(
        [projection_part.reshape(shards, rows, width), gain_rows.astype(jnp.bfloat16)], 1
    )
    side = lax.axis_index("shard")
    packed = [
        lax.dynamic_index_in_dim(packed, lax.rem(side + step, shards), 0, keepdims=False).astype(
            jnp.float32
        )
        for step in range(shards)
    ]
    *ffn_sums, packed = lax.psum((*ffn_own, returned(packed, shards)), "replica")
    packed = packed.astype(jnp.float32)
    gate_grad, up_grad, down_grad = [total.astype(jnp.float32) for total in ffn_sums]
    ends = [query_size, query_size + key_size, query_size + 2 * key_size]
    query_grad = packed[:rows, : ends[0]]
    key_grad = packed[:rows, ends[0] : ends[1]]
    value_grad = packed[:rows, ends[1] : ends[2]]
    output_grad = packed[:rows, ends[2] :]
    gain_one_grad = packed[rows, :rows]
    gain_two_grad = packed[rows, rows : 2 * rows]
    return (
        layer_output,
        input_grad,
        gain_one_grad,
        query_grad,
        key_grad,
        value_grad,
        output_grad,
        gain_two_grad,
        gate_grad,
        up_grad,
        down_grad,
    )


def solution(mesh):
    placed = (
        P(("replica", "shard"), None),
        P(("replica", "shard"), None),
        P(("replica", "shard"), None),
        P("shard"),
        P("shard", None),
        P("shard", None),
        P("shard", None),
        P("shard", None),
        P("shard"),
        P(None, "shard"),
        P(None, "shard"),
        P("shard", None),
    )
    return jax.shard_map(
        functools.partial(per_device, mesh.shape["shard"]),
        mesh=mesh,
        in_specs=placed,
        out_specs=(
            P(("replica", "shard"), None),
            P(("replica", "shard"), None),
            P("shard"),
            P("shard", None),
            P("shard", None),
            P("shard", None),
            P("shard", None),
            P("shard"),
            P(None, "shard"),
            P(None, "shard"),
            P("shard", None),
        ),
        check_vma=False,
    )
```
